512 devices in a mesh: rep: 32 (over x_lo, z), fsdp: 16 (over y, x_hi, core).
Axes of the slice: x: 4 (x_hi: 2, x_lo: 2; x = x_hi * 2 + x_lo), y: 4, z: 16, core: 2. Of those that a mesh axis runs over, the one named last changes fastest.
Arguments:
- master: float32 [32, 8192, 512], P('rep', 'fsdp'), may hold values from -6 to 6
- features: bfloat16 [32, 2048, 8192], P('rep', 'fsdp'), may hold values from -6 to 6
- targets: bfloat16 [32, 2048, 512], P('rep', 'fsdp'), may hold values from -6 to 6
Outputs:
- updated: float32 [32, 8192, 512], P('rep', 'fsdp')
The draws below stay inside these ranges and needn't reach their ends.
All inputs are finite; a program needn't handle non-finite values.
Results may differ from the reference program's by a relative error of at most 0.0024.
Values may be sent and summed in bfloat16 or wider, within the bound.
No kernel may reach another device: no remote copies, remote signals or barrier semaphores. Data moves between devices by JAX's collectives and lax.ppermute only.
A program may use at most 64 MiB of HBM per device.

```python
import jax
import jax.numpy as jnp
from jax import lax

D = 8192
KVW = 512
STEP = 3
TOKENS = 2048
REPS = 32
N_REP = 32


def block_levels(rng, extent, shards, least, high):
    gain, own = 1.0, jax.random.fold_in(rng, 6)
    for dim, blocks in shards:
        heights = jnp.exp(jax.random.uniform(jax.random.fold_in(own, dim), (blocks,), jnp.float32, least / len(shards), high / len(shards)))
        gain = gain * jnp.repeat(heights, extent[dim] // blocks).reshape([-1 if axis == dim else 1 for axis in range(len(extent))])
    return gain


def bell_draw(key, extent, spread, reach, pieces=(), kind=jnp.bfloat16):
    loudness = block_levels(key, extent, pieces, -0.22, 0.18) if pieces else 1.0
    array = jax.random.normal(key, extent, jnp.float32) * spread * loudness
    return jnp.minimum(jnp.maximum(array, -reach), reach).astype(kind)


def setup_inputs(seed: int = 0) -> dict:
    arg_keys = jax.random.split(jax.random.key(seed), 4)
    return {
        "master": bell_draw(arg_keys[0], (REPS, D, KVW), 1.0, 6.0, ((0, 32), (1, 16)), jnp.float32),
        "features": bell_draw(arg_keys[1], (REPS, TOKENS, D), 1.0, 6.0, ((0, 32), (1, 16))),
        "targets": bell_draw(arg_keys[2], (REPS, TOKENS, KVW), 1.0, 6.0, ((0, 32), (1, 16))),
    }


def one_replica(inputs):
    master, features, targets = inputs
    scale = 1.0 / (D ** 0.5)
    working = master.astype(jnp.bfloat16).astype(jnp.float32)
    feats = features.astype(jnp.float32)
    keys = jnp.dot(feats, working, precision=lax.Precision.HIGHEST) * scale
    error = (keys - targets.astype(jnp.float32)).astype(jnp.bfloat16).astype(jnp.float32)
    grad = jnp.dot(feats.T, error, precision=lax.Precision.HIGHEST) * scale
    return master - 0.5 * grad


def reference(master, features, targets):
    stepped = lax.map(one_replica, (master, features, targets))
    levels = N_REP.bit_length() - 1
    hop = 2 ** (STEP % levels)
    return 0.5 * (stepped + jnp.roll(stepped, hop, axis=0))
```

```python
import jax
import jax.numpy as jnp
from jax import lax
from jax.sharding import PartitionSpec as P

D = 8192
STEP = 3
CHUNKS = 4


def from_behind(block, axis, distance):
    devices = range(lax.axis_size(axis))
    route = [((i - distance) % len(devices), i) for i in devices]
    return lax.ppermute(block, axis, route)


def body(master, features, targets):
    scale = 1.0 / D**0.5
    levels = lax.axis_size("rep").bit_length() - 1
    hop = 2 ** (STEP % levels)
    size = lax.axis_size("fsdp")
    chips = size // 2
    core = lax.axis_index("fsdp") % 2
    groups = [list(range(c, size, 2)) for c in range(2)]
    swap_route = [(i, i ^ 1) for i in range(size)]

    def exchange(blocks):
        return lax.all_to_all(blocks, "fsdp", 0, 0, axis_index_groups=groups)

    def swap(block):
        return lax.ppermute(block, "fsdp", swap_route)

    own_master = master[0]
    rows, width = own_master.shape
    tokens = features[0]
    count = tokens.shape[0]
    depth = 2 * rows

    working = own_master.astype(jnp.bfloat16)
    peer = swap(working)
    first = jnp.where(core == 0, working, peer)
    second = jnp.where(core == 0, peer, working)
    weights = jnp.concatenate([first, second], axis=0)

    columns = exchange(tokens.reshape(count, chips, depth).transpose(1, 0, 2))
    columns = columns.reshape(chips * count, depth)

    step = width // CHUNKS
    results = []
    for c in range(CHUNKS):
        part = slice(c * step, (c + 1) * step)
        partial = jnp.dot(columns, weights[:, part], preferred_element_type=jnp.float32)
        partial = (partial * scale).astype(jnp.bfloat16).reshape(chips, count, step)
        keys = exchange(partial).astype(jnp.float32).sum(axis=0)
        error = (keys - targets[0][:, part].astype(jnp.float32)).astype(jnp.bfloat16)
        errors = exchange(jnp.broadcast_to(error, (chips, count, step)))
        grad = lax.dot_general(
            columns,
            errors.reshape(chips * count, step),
            (((0,), (0,)), ((), ())),
            preferred_element_type=jnp.float32,
        ).reshape(2, rows, step)
        kept = lax.dynamic_index_in_dim(grad, core, 0, keepdims=False)
        given = lax.dynamic_index_in_dim(grad, 1 - core, 0, keepdims=False)
        grad = kept + swap(given)
        stepped = own_master[:, part] - (0.5 * scale) * grad
        other = from_behind(stepped.astype(jnp.bfloat16), "rep", hop)
        results.append(0.5 * (stepped + other.astype(jnp.float32)))
    return jnp.concatenate(results, axis=1)[None]


def solution(mesh):
    return jax.shard_map(
        body,
        mesh=mesh,
        in_specs=(P("rep", "fsdp", None), P("rep", "fsdp", None), P("rep", "fsdp", None)),
        out_specs=P("rep", "fsdp", None),
        check_vma=False,
    )
```

```python
import functools

import jax
import jax.numpy as jnp
from jax import lax
from jax.experimental import pallas as pl
from jax.experimental.pallas import tpu as pltpu
from jax.sharding import PartitionSpec as P

D = 8192
STEP = 3
HALVES = 2
SCALE = 1.0 / D**0.5

VMEM = pl.BlockSpec(memory_space=pltpu.VMEM)
ANY = pl.BlockSpec(memory_space=pl.ANY)
F32 = jnp.float32
BF16 = jnp.bfloat16


def call(kernel, name, outs, ins, spec=VMEM, aliases=None):
    return pl.pallas_call(
        kernel,
        name=name,
        out_shape=[jax.ShapeDtypeStruct(s, d) for s, d in outs],
        in_specs=list(ins),
        out_specs=[spec] * len(outs),
        input_output_aliases=aliases or {},
        compiler_params=pltpu.CompilerParams(vmem_limit_bytes=8 * 1024 * 1024),
        cost_estimate=pl.CostEstimate(flops=1_000_000, bytes_accessed=1_000_000, transcendentals=0),
    )


def round_kernel(master, working):
    working[...] = master[...].astype(BF16)


def block_kernel(features, _, blocks):
    core = lax.rem(lax.axis_index("fsdp"), 2)
    chips, _, _, rows = blocks.shape
    for q in range(chips):
        for h, half in enumerate((core, 1 - core)):
            start = pl.multiple_of(q * 2 * rows + half * rows, rows)
            blocks[q, h] = features[:, pl.ds(start, rows)]


def after_kernel(*_):
    pass


def keys_kernel(blocks, own, peer, out):
    chips, _, count, rows = blocks.shape
    first = blocks[:, 0].reshape(chips * count, rows)
    second = blocks[:, 1].reshape(chips * count, rows)
    for c in range(0, own.shape[1], 256):
        part = slice(c, c + 256)
        total = jnp.dot(first, own[:, part], preferred_element_type=F32)
        total += jnp.dot(second, peer[:, part], preferred_element_type=F32)
        out[:, :, part] = (total * SCALE).astype(BF16).reshape(chips, count, 256)


def error_kernel(parts, targets, out):
    for c in range(0, out.shape[2], 128):
        part = slice(c, c + 128)
        keys = parts[0, :, part].astype(F32)
        for q in range(1, parts.shape[0]):
            keys += parts[q, :, part].astype(F32)
        error = (keys - targets[:, part].astype(F32)).astype(BF16)
        for q in range(out.shape[0]):
            out[q, :, part] = error


def grad_kernel(k, start, stop, blocks, errors, *rest):
    chips, _, count, rows = blocks.shape
    grad = lax.dot_general(
        blocks[:, k].reshape(chips * count, rows),
        errors[:, :, start:stop].reshape(chips * count, stop - start),
        (((0,), (0,)), ((), ())),
        preferred_element_type=F32,
    )
    rest[-1][...] = grad.astype(rest[-1].dtype)


def step_kernel(start, stop, kept, given, master, stepped, sent):
    new = master[:, start:stop] - (0.5 * SCALE) * (kept[...] + given[...].astype(F32))
    stepped[...] = new
    sent[...] = new.astype(BF16)


def average_kernel(chunks, *refs):
    out = refs[-1]
    for i, (start, stop) in enumerate(chunks):
        out[:, start:stop] = 0.5 * (refs[2 * i][...] + refs[2 * i + 1][...].astype(F32))


def from_behind(block, axis, distance):
    devices = range(lax.axis_size(axis))
    route = [((i - distance) % len(devices), i) for i in devices]
    return lax.ppermute(block, axis, route)


def body(master, features, targets):
    levels = lax.axis_size("rep").bit_length() - 1
    hop = 2 ** (STEP % levels)
    size = lax.axis_size("fsdp")
    chips = size // 2
    groups = [list(range(c, size, 2)) for c in range(2)]
    swap_route = [(i, i ^ 1) for i in range(size)]

    def exchange(blocks):
        return lax.all_to_all(blocks, "fsdp", 0, 0, axis_index_groups=groups)

    def swap(block):
        return lax.ppermute(block, "fsdp", swap_route)

    master, tokens, targets = master[0], features[0], targets[0]
    rows, width = master.shape
    count = tokens.shape[0]
    part = width // HALVES
    chunks = [(h * part, (h + 1) * part) for h in range(HALVES)]

    (working,) = call(round_kernel, "round", [((rows, width), BF16)], [VMEM])(master)
    peer = swap(working)
    shape = (chips, 2, count, rows)
    (blocks,) = call(block_kernel, "block", [(shape, BF16)], [VMEM, ANY])(tokens, working)
    (blocks,) = call(after_kernel, "after", [(shape, BF16)], [ANY] * 2, ANY, {0: 0})(blocks, peer)
    blocks = exchange(blocks)

    shape = (chips, count, width)
    (partial,) = call(keys_kernel, "keys", [(shape, BF16)], [VMEM] * 3)(blocks, working, peer)
    (error,) = call(error_kernel, "error", [(shape, BF16)], [VMEM] * 2)(exchange(partial), targets)
    errors = exchange(error)

    results, given, after = [], [], []
    for h, (start, stop) in enumerate(chunks):
        (term,) = call(
            functools.partial(grad_kernel, 1, start, stop),
            f"given_{h}",
            [((rows, part), BF16)],
            [VMEM] * 2 + [ANY] * len(after),
        )(blocks, errors, *after)
        after = [term]
        given.append(swap(term))
    for h, (start, stop) in enumerate(chunks):
        (kept,) = call(
            functools.partial(grad_kernel, 0, start, stop),
            f"kept_{h}",
            [((rows, part), F32)],
            [VMEM] * 2 + [ANY] * len(after),
        )(blocks, errors, *after)
        stepped, sent = call(
            functools.partial(step_kernel, start, stop),
            f"step_{h}",
            [((rows, part), F32), ((rows, part), BF16)],
            [VMEM] * 3,
        )(kept, given[h], master)
        after = [kept]
        results += [stepped, from_behind(sent, "rep", hop)]
    (updated,) = call(
        functools.partial(average_kernel, chunks),
        "average",
        [((rows, width), F32)],
        [VMEM] * len(results),
    )(*results)
    return updated[None]


def solution(mesh):
    return jax.shard_map(
        body,
        mesh=mesh,
        in_specs=(P("rep", "fsdp", None), P("rep", "fsdp", None), P("rep", "fsdp", None)),
        out_specs=P("rep", "fsdp", None),
        check_vma=False,
    )
```

```python
import functools

import jax
import jax.numpy as jnp
from jax import lax
from jax.experimental import pallas as pl
from jax.experimental.pallas import tpu as pltpu
from jax.sharding import PartitionSpec as P

D = 8192
STEP = 3
PIECES = (256, 256)
SIDE = 4
SCALE = 1.0 / D**0.5

VMEM = pl.BlockSpec(memory_space=pltpu.VMEM)
ANY = pl.BlockSpec(memory_space=pl.ANY)
F32 = jnp.float32
BF16 = jnp.bfloat16


def call(kernel, name, outs, ins, scratch=()):
    return pl.pallas_call(
        kernel,
        name=name,
        out_shape=[jax.ShapeDtypeStruct(s, d) for s, d in outs],
        in_specs=list(ins),
        out_specs=[VMEM] * len(outs),
        scratch_shapes=list(scratch),
        compiler_params=pltpu.CompilerParams(vmem_limit_bytes=8 * 1024 * 1024),
        cost_estimate=pl.CostEstimate(flops=1_000_000, bytes_accessed=1_000_000, transcendentals=0),
    )


def round_kernel(master, working):
    working[...] = master[...].astype(BF16)


def block_kernel(features, blocks):
    mine = lax.rem(lax.axis_index("fsdp"), SIDE)
    ring, _, _, rows = blocks.shape
    for k in range(SIDE):
        for y in range(ring):
            start = pl.multiple_of((y * SIDE + (mine ^ k)) * rows, rows)
            blocks[y, k] = features[:, pl.ds(start, rows)]


def keys_kernel(blocks, *refs):
    *sources, out, working, sem = refs
    ring, _, count, rows = blocks.shape
    copies = [
        pltpu.make_async_copy(source, working.at[k], sem.at[k]) for k, source in enumerate(sources)
    ]
    for copy in copies:
        copy.start()
    for copy in copies:
        copy.wait()
    for c in range(0, out.shape[2], 256):
        part = slice(c, c + 256)
        total = sum(
            jnp.dot(
                blocks[:, k].reshape(ring * count, rows),
                working[k, :, part],
                preferred_element_type=F32,
            )
            for k in range(SIDE)
        )
        out[:, :, part] = (total * SCALE).astype(BF16).reshape(ring, count, 256)


def error_kernel(parts, targets, out):
    for c in range(0, out.shape[2], 128):
        part = slice(c, c + 128)
        keys = parts[0, :, part].astype(F32)
        for q in range(1, parts.shape[0]):
            keys += parts[q, :, part].astype(F32)
        error = (keys - targets[:, part].astype(F32)).astype(BF16)
        for q in range(out.shape[0]):
            out[q, :, part] = error


def term(blocks, errors, k, start, stop):
    ring, _, count, rows = blocks.shape
    return lax.dot_general(
        blocks[:, k].reshape(ring * count, rows),
        errors[:, :, start:stop].reshape(ring * count, stop - start),
        (((0,), (0,)), ((), ())),
        preferred_element_type=F32,
    )


def given_kernel(start, stop, blocks, errors, out):
    for i, k in enumerate((3, 1)):
        out[i] = term(blocks, errors, k, start, stop).astype(BF16)


def kept_kernel(start, stop, blocks, errors, _, across, own):
    across[...] = term(blocks, errors, 2, start, stop)
    own[...] = term(blocks, errors, 0, start, stop)


def across_kernel(kept, given, out):
    out[...] = (kept[...] + given[0].astype(F32)).astype(BF16)


def step_kernel(start, stop, kept, given, crossed, master, stepped, sent):
    grad = kept[...] + given[1].astype(F32) + crossed[...].astype(F32)
    new = master[:, start:stop] - (0.5 * SCALE) * grad
    stepped[...] = new
    sent[...] = new.astype(BF16)


def average_kernel(chunks, *refs):
    out = refs[-1]
    for i, (start, stop) in enumerate(chunks):
        out[:, start:stop] = 0.5 * (refs[2 * i][...] + refs[2 * i + 1][...].astype(F32))


def from_behind(block, axis, distance):
    devices = range(lax.axis_size(axis))
    route = [((i - distance) % len(devices), i) for i in devices]
    return lax.ppermute(block, axis, route)


def body(master, features, targets):
    levels = lax.axis_size("rep").bit_length() - 1
    hop = 2 ** (STEP % levels)
    size = lax.axis_size("fsdp")
    ring = size // SIDE
    groups = [list(range(k, size, SIDE)) for k in range(SIDE)]

    def exchange(blocks):
        return lax.all_to_all(blocks, "fsdp", 0, 0, axis_index_groups=groups)

    def swap(block, k):
        return lax.ppermute(block, "fsdp", [(i, i ^ k) for i in range(size)])

    master, tokens, targets = master[0], features[0], targets[0]
    rows, width = master.shape
    count = tokens.shape[0]
    edges = [sum(PIECES[:h]) for h in range(len(PIECES) + 1)]
    chunks = list(zip(edges[:-1], edges[1:]))

    (working,) = call(round_kernel, "round", [((rows, width), BF16)], [VMEM])(master)
    beside = swap(working, 1)
    across = swap(working, 2)
    working = [working, beside, across, swap(across, 1)]
    shape = (ring, SIDE, count, rows)
    (blocks,) = call(block_kernel, "block", [(shape, BF16)], [VMEM])(tokens)
    blocks = exchange(blocks)

    shape = (ring, count, width)
    (partial,) = call(
        keys_kernel,
        "keys",
        [(shape, BF16)],
        [VMEM] + [ANY] * SIDE,
        scratch=[pltpu.VMEM((SIDE, rows, width), BF16), pltpu.SemaphoreType.DMA((SIDE,))],
    )(blocks, *working)
    (error,) = call(error_kernel, "error", [(shape, BF16)], [VMEM] * 2)(exchange(partial), targets)
    errors = exchange(error)

    results = []
    for h, (start, stop) in enumerate(chunks):
        half = (rows, stop - start)
        (given,) = call(
            functools.partial(given_kernel, start, stop),
            f"given_{h}",
            [((2, *half), BF16)],
            [VMEM] * 2,
        )(blocks, errors)
        across, kept = call(
            functools.partial(kept_kernel, start, stop),
            f"kept_{h}",
            [(half, F32)] * 2,
            [VMEM] * 2 + [ANY],
        )(blocks, errors, given)
        given = swap(given, 1)
        (across,) = call(across_kernel, f"across_{h}", [(half, BF16)], [VMEM] * 2)(across, given)
        stepped, sent = call(
            functools.partial(step_kernel, start, stop),
            f"step_{h}",
            [(half, F32), (half, BF16)],
            [VMEM] * 4,
        )(kept, given, swap(across, 2), master)
        results += [stepped, from_behind(sent, "rep", hop)]
    (updated,) = call(
        functools.partial(average_kernel, chunks),
        "average",
        [((rows, width), F32)],
        [VMEM] * len(results),
    )(*results)
    return updated[None]


def solution(mesh):
    return jax.shard_map(
        body,
        mesh=mesh,
        in_specs=(P("rep", "fsdp", None), P("rep", "fsdp", None), P("rep", "fsdp", None)),
        out_specs=P("rep", "fsdp", None),
        check_vma=False,
    )
```

```python
import functools

import jax
import jax.numpy as jnp
from jax import lax
from jax.experimental import pallas as pl
from jax.experimental.pallas import tpu as pltpu
from jax.sharding import PartitionSpec as P

D = 8192
STEP = 3
PIECES = (256, 256)
SIDE = 4
SCALE = 1.0 / D**0.5

VMEM = pl.BlockSpec(memory_space=pltpu.VMEM)
ANY = pl.BlockSpec(memory_space=pl.ANY)
F32 = jnp.float32
BF16 = jnp.bfloat16


def call(kernel, name, outs, ins):
    return pl.pallas_call(
        kernel,
        name=name,
        out_shape=[jax.ShapeDtypeStruct(s, d) for s, d in outs],
        in_specs=list(ins),
        out_specs=[VMEM] * len(outs),
        compiler_params=pltpu.CompilerParams(vmem_limit_bytes=8 * 1024 * 1024),
        cost_estimate=pl.CostEstimate(flops=1_000_000, bytes_accessed=1_000_000, transcendentals=0),
    )


def round_kernel(master, working):
    working[...] = master[...].astype(BF16)


def block_kernel(features, blocks):
    mine = lax.rem(lax.axis_index("fsdp"), SIDE)
    ring, _, _, rows = blocks.shape
    for k in range(SIDE):
        for y in range(ring):
            start = pl.multiple_of((y * SIDE + (mine ^ k)) * rows, rows)
            blocks[y, k] = features[:, pl.ds(start, rows)]


def stack_kernel(*refs):
    *sources, out = refs
    for k, source in enumerate(sources):
        out[k] = source[...]


def keys_kernel(blocks, working, out):
    ring, _, count, rows = blocks.shape
    for c in range(0, out.shape[2], 256):
        part = slice(c, c + 256)
        total = sum(
            jnp.dot(
                blocks[:, k].reshape(ring * count, rows),
                working[k, :, part],
                preferred_element_type=F32,
            )
            for k in range(SIDE)
        )
        out[:, :, part] = (total * SCALE).astype(BF16).reshape(ring, count, 256)


def error_kernel(parts, targets, out):
    for c in range(0, out.shape[2], 128):
        part = slice(c, c + 128)
        keys = parts[0, :, part].astype(F32)
        for q in range(1, parts.shape[0]):
            keys += parts[q, :, part].astype(F32)
        error = (keys - targets[:, part].astype(F32)).astype(BF16)
        for q in range(out.shape[0]):
            out[q, :, part] = error


def term(blocks, errors, k, start, stop):
    ring, _, count, rows = blocks.shape
    return lax.dot_general(
        blocks[:, k].reshape(ring * count, rows),
        errors[:, :, start:stop].reshape(ring * count, stop - start),
        (((0,), (0,)), ((), ())),
        preferred_element_type=F32,
    )


def given_kernel(start, stop, blocks, errors, out):
    for i, k in enumerate((3, 1)):
        out[i] = term(blocks, errors, k, start, stop).astype(BF16)


def kept_kernel(start, stop, blocks, errors, _, across, own):
    across[...] = term(blocks, errors, 2, start, stop)
    own[...] = term(blocks, errors, 0, start, stop)


def across_kernel(kept, given, out):
    out[...] = (kept[...] + given[0].astype(F32)).astype(BF16)


def step_kernel(start, stop, kept, given, crossed, master, stepped, sent):
    grad = kept[...] + given[1].astype(F32) + crossed[...].astype(F32)
    new = master[:, start:stop] - (0.5 * SCALE) * grad
    stepped[...] = new
    sent[...] = new.astype(BF16)


def average_kernel(chunks, *refs):
    out = refs[-1]
    for i, (start, stop) in enumerate(chunks):
        out[:, start:stop] = 0.5 * (refs[2 * i][...] + refs[2 * i + 1][...].astype(F32))


def from_behind(block, axis, distance):
    devices = range(lax.axis_size(axis))
    route = [((i - distance) % len(devices), i) for i in devices]
    return lax.ppermute(block, axis, route)


def body(master, features, targets):
    levels = lax.axis_size("rep").bit_length() - 1
    hop = 2 ** (STEP % levels)
    size = lax.axis_size("fsdp")
    ring = size // SIDE
    groups = [list(range(k, size, SIDE)) for k in range(SIDE)]

    def exchange(blocks):
        return lax.all_to_all(blocks, "fsdp", 0, 0, axis_index_groups=groups)

    def swap(block, k):
        return lax.ppermute(block, "fsdp", [(i, i ^ k) for i in range(size)])

    master, tokens, targets = master[0], features[0], targets[0]
    rows, width = master.shape
    count = tokens.shape[0]
    edges = [sum(PIECES[:h]) for h in range(len(PIECES) + 1)]
    chunks = list(zip(edges[:-1], edges[1:]))

    (working,) = call(round_kernel, "round", [((rows, width), BF16)], [VMEM])(master)
    beside = swap(working, 1)
    across = swap(working, 2)
    (working,) = call(stack_kernel, "stack", [((SIDE, rows, width), BF16)], [VMEM] * SIDE)(
        working, beside, across, swap(across, 1)
    )
    shape = (ring, SIDE, count, rows)
    (blocks,) = call(block_kernel, "block", [(shape, BF16)], [VMEM])(tokens)
    blocks = exchange(blocks)

    shape = (ring, count, width)
    (partial,) = call(keys_kernel, "keys", [(shape, BF16)], [VMEM] * 2)(blocks, working)
    (error,) = call(error_kernel, "error", [(shape, BF16)], [VMEM] * 2)(exchange(partial), targets)
    errors = exchange(error)

    results = []
    for h, (start, stop) in enumerate(chunks):
        half = (rows, stop - start)
        (given,) = call(
            functools.partial(given_kernel, start, stop),
            f"given_{h}",
            [((2, *half), BF16)],
            [VMEM] * 2,
        )(blocks, errors)
        across, kept = call(
            functools.partial(kept_kernel, start, stop),
            f"kept_{h}",
            [(half, F32)] * 2,
            [VMEM] * 2 + [ANY],
        )(blocks, errors, given)
        given = swap(given, 1)
        (across,) = call(across_kernel, f"across_{h}", [(half, BF16)], [VMEM] * 2)(across, given)
        stepped, sent = call(
            functools.partial(step_kernel, start, stop),
            f"step_{h}",
            [(half, F32), (half, BF16)],
            [VMEM] * 4,
        )(kept, given, swap(across, 2), master)
        results += [stepped, from_behind(sent, "rep", hop)]
    (updated,) = call(
        functools.partial(average_kernel, chunks),
        "average",
        [((rows, width), F32)],
        [VMEM] * len(results),
    )(*results)
    return updated[None]


def solution(mesh):
    return jax.shard_map(
        body,
        mesh=mesh,
        in_specs=(P("rep", "fsdp", None), P("rep", "fsdp", None), P("rep", "fsdp", None)),
        out_specs=P("rep", "fsdp", None),
        check_vma=False,
    )
```

```python
import functools

import jax
import jax.numpy as jnp
from jax import lax
from jax.experimental import pallas as pl
from jax.experimental.pallas import tpu as pltpu
from jax.sharding import PartitionSpec as P

D = 8192
STEP = 3
PIECES = (256, 256)
FLOPS = 10_000_000_000
KEPT = (1_000_000, 10_000_000_000)
SIDE = 4
SCALE = 1.0 / D**0.5

VMEM = pl.BlockSpec(memory_space=pltpu.VMEM)
ANY = pl.BlockSpec(memory_space=pl.ANY)
F32 = jnp.float32
BF16 = jnp.bfloat16


def call(kernel, name, outs, ins, flops=1_000_000):
    return pl.pallas_call(
        kernel,
        name=name,
        out_shape=[jax.ShapeDtypeStruct(s, d) for s, d in outs],
        in_specs=list(ins),
        out_specs=[VMEM] * len(outs),
        compiler_params=pltpu.CompilerParams(vmem_limit_bytes=8 * 1024 * 1024),
        cost_estimate=pl.CostEstimate(flops=flops, bytes_accessed=1_000_000, transcendentals=0),
    )


def round_kernel(master, working):
    working[...] = master[...].astype(BF16)


def block_kernel(features, blocks, held, sem):
    mine = lax.rem(lax.axis_index("fsdp"), SIDE)
    ring, _, _, rows = blocks.shape
    places = [(y, k) for y in range(ring) for k in range(SIDE)]
    reads, writes = [], []
    for y, k in places:
        start = pl.multiple_of((y * SIDE + (mine ^ k)) * rows, rows)
        source = features.at[:, pl.ds(start, rows)]
        reads.append(pltpu.make_async_copy(source, held.at[y, k], sem.at[0, y, k]))
        writes.append(pltpu.make_async_copy(held.at[y, k], blocks.at[y, k], sem.at[1, y, k]))
        reads[-1].start()
    for read, write in zip(reads, writes):
        read.wait()
        write.start()
    for write in writes:
        write.wait()


def stack_kernel(*refs):
    *sources, out = refs
    for k, source in enumerate(sources):
        out[k] = source[...]


def keys_kernel(blocks, working, out):
    ring, _, count, rows = blocks.shape
    for c in range(0, out.shape[2], 256):
        part = slice(c, c + 256)
        total = sum(
            jnp.dot(
                blocks[:, k].reshape(ring * count, rows),
                working[k, :, part],
                preferred_element_type=F32,
            )
            for k in range(SIDE)
        )
        out[:, :, part] = (total * SCALE).astype(BF16).reshape(ring, count, 256)


def error_kernel(parts, targets, out):
    for c in range(0, out.shape[2], 128):
        part = slice(c, c + 128)
        keys = parts[0, :, part].astype(F32)
        for q in range(1, parts.shape[0]):
            keys += parts[q, :, part].astype(F32)
        error = (keys - targets[:, part].astype(F32)).astype(BF16)
        for q in range(out.shape[0]):
            out[q, :, part] = error


def term(blocks, errors, k, start, stop):
    ring, _, count, rows = blocks.shape
    return lax.dot_general(
        blocks[:, k].reshape(ring * count, rows),
        errors[:, :, start:stop].reshape(ring * count, stop - start),
        (((0,), (0,)), ((), ())),
        preferred_element_type=F32,
    )


def given_kernel(start, stop, blocks, errors, *rest):
    out = rest[-1]
    for i, k in enumerate((3, 1)):
        out[i] = term(blocks, errors, k, start, stop).astype(BF16)


def kept_kernel(start, stop, blocks, errors, _, across, own):
    across[...] = term(blocks, errors, 2, start, stop)
    own[...] = term(blocks, errors, 0, start, stop)


def across_kernel(kept, given, out):
    out[...] = (kept[...] + given[0].astype(F32)).astype(BF16)


def step_kernel(start, stop, kept, given, crossed, master, stepped, sent):
    grad = kept[...] + given[1].astype(F32) + crossed[...].astype(F32)
    new = master[:, start:stop] - (0.5 * SCALE) * grad
    stepped[...] = new
    sent[...] = new.astype(BF16)


def mean_kernel(stepped, other, out):
    out[...] = 0.5 * (stepped[...] + other[...].astype(F32))


def average_kernel(*refs):
    *means, stepped, other, out = refs
    start = 0
    for mean in means:
        stop = start + mean.shape[1]
        out[:, start:stop] = mean[...]
        start = stop
    out[:, start:] = 0.5 * (stepped[...] + other[...].astype(F32))


def from_behind(block, axis, distance):
    devices = range(lax.axis_size(axis))
    route = [((i - distance) % len(devices), i) for i in devices]
    return lax.ppermute(block, axis, route)


def body(master, features, targets):
    levels = lax.axis_size("rep").bit_length() - 1
    hop = 2 ** (STEP % levels)
    size = lax.axis_size("fsdp")
    ring = size // SIDE
    groups = [list(range(k, size, SIDE)) for k in range(SIDE)]

    def exchange(blocks):
        return lax.all_to_all(blocks, "fsdp", 0, 0, axis_index_groups=groups)

    def swap(block, k):
        return lax.ppermute(block, "fsdp", [(i, i ^ k) for i in range(size)])

    master, tokens, targets = master[0], features[0], targets[0]
    rows, width = master.shape
    count = tokens.shape[0]
    edges = [sum(PIECES[:h]) for h in range(len(PIECES) + 1)]
    chunks = list(zip(edges[:-1], edges[1:]))

    (working,) = call(round_kernel, "round", [((rows, width), BF16)], [VMEM])(master)
    beside = swap(working, 1)
    across = swap(working, 2)
    (working,) = call(stack_kernel, "stack", [((SIDE, rows, width), BF16)], [VMEM] * SIDE)(
        working, beside, across, swap(across, 1)
    )
    shape = (ring, SIDE, count, rows)
    blocks = pl.pallas_call(
        block_kernel,
        name="block",
        out_shape=jax.ShapeDtypeStruct(shape, BF16),
        in_specs=[pl.BlockSpec(memory_space=pl.ANY)],
        out_specs=pl.BlockSpec(memory_space=pl.ANY),
        scratch_shapes=[pltpu.VMEM(shape, BF16), pltpu.SemaphoreType.DMA((2, ring, SIDE))],
        compiler_params=pltpu.CompilerParams(vmem_limit_bytes=60 * 1024 * 1024),
    )(tokens)
    blocks = exchange(blocks)

    shape = (ring, count, width)
    (partial,) = call(keys_kernel, "keys", [(shape, BF16)], [VMEM] * 2)(blocks, working)
    (error,) = call(error_kernel, "error", [(shape, BF16)], [VMEM] * 2)(exchange(partial), targets)
    errors = exchange(error)

    results, after = [], []
    for h, (start, stop) in enumerate(chunks):
        half = (rows, stop - start)
        weight = max((len(chunks) - 1 - h) * FLOPS, 1_000_000)
        mean_weight = weight if len(chunks) == 2 else 1_000_000
        (given,) = call(
            functools.partial(given_kernel, start, stop),
            f"given_{h}",
            [((2, *half), BF16)],
            [VMEM] * 2 + [ANY] * len(after),
        )(blocks, errors, *after)
        across, kept = call(
            functools.partial(kept_kernel, start, stop),
            f"kept_{h}",
            [(half, F32)] * 2,
            [VMEM] * 2 + [ANY],
            KEPT[h],
        )(blocks, errors, given)
        given = swap(given, 1)
        (across,) = call(across_kernel, f"across_{h}", [(half, BF16)], [VMEM] * 2, weight)(
            across, given
        )
        after = [across]
        stepped, sent = call(
            functools.partial(step_kernel, start, stop),
            f"step_{h}",
            [(half, F32), (half, BF16)],
            [VMEM] * 4,
            weight,
        )(kept, given, swap(across, 2), master)
        result = (stepped, from_behind(sent, "rep", hop))
        if h < len(chunks) - 1:
            result = call(mean_kernel, f"mean_{h}", [(half, F32)], [VMEM] * 2, mean_weight)(*result)
        results += result
    (updated,) = call(average_kernel, "average", [((rows, width), F32)], [VMEM] * len(results))(
        *results
    )
    return updated[None]


def solution(mesh):
    return jax.shard_map(
        body,
        mesh=mesh,
        in_specs=(P("rep", "fsdp", None), P("rep", "fsdp", None), P("rep", "fsdp", None)),
        out_specs=P("rep", "fsdp", None),
        check_vma=False,
    )
```

```python
import functools

import jax
import jax.numpy as jnp
from jax import lax
from jax.experimental import pallas as pl
from jax.experimental.pallas import tpu as pltpu
from jax.sharding import PartitionSpec as P

D = 8192
STEP = 3
PIECES = (256, 256)
FLOPS = 10_000_000_000
KEPT = (1_000_000, 10_000_000_000)
SIDE = 4
SCALE = 1.0 / D**0.5

VMEM = pl.BlockSpec(memory_space=pltpu.VMEM)
ANY = pl.BlockSpec(memory_space=pl.ANY)
F32 = jnp.float32
BF16 = jnp.bfloat16


def call(kernel, name, outs, ins, flops=1_000_000):
    return pl.pallas_call(
        kernel,
        name=name,
        out_shape=[jax.ShapeDtypeStruct(s, d) for s, d in outs],
        in_specs=list(ins),
        out_specs=[VMEM] * len(outs),
        compiler_params=pltpu.CompilerParams(vmem_limit_bytes=8 * 1024 * 1024),
        cost_estimate=pl.CostEstimate(flops=flops, bytes_accessed=1_000_000, transcendentals=0),
    )


def round_kernel(master, working):
    working[...] = master[...].astype(BF16)


def block_kernel(features, blocks, held, sem):
    mine = lax.rem(lax.axis_index("fsdp"), SIDE)
    ring, _, _, rows = blocks.shape
    reads, writes = [], []
    for y in range(ring):
        source = features.at[:, pl.ds(y * SIDE * rows, SIDE * rows)]
        reads.append(pltpu.make_async_copy(source, held.at[y], sem.at[0, y, 0]))
        reads[-1].start()
    for y in range(ring):
        reads[y].wait()
        for k in range(SIDE):
            start = pl.multiple_of((mine ^ k) * rows, rows)
            source = held.at[y, :, pl.ds(start, rows)]
            writes.append(pltpu.make_async_copy(source, blocks.at[y, k], sem.at[1, y, k]))
            writes[-1].start()
    for write in writes:
        write.wait()


def stack_kernel(*refs):
    *sources, out = refs
    for k, source in enumerate(sources):
        out[k] = source[...]


def keys_kernel(blocks, working, out):
    ring, _, count, rows = blocks.shape
    for c in range(0, out.shape[2], 256):
        part = slice(c, c + 256)
        total = sum(
            jnp.dot(
                blocks[:, k].reshape(ring * count, rows),
                working[k, :, part],
                preferred_element_type=F32,
            )
            for k in range(SIDE)
        )
        out[:, :, part] = (total * SCALE).astype(BF16).reshape(ring, count, 256)


def error_kernel(parts, targets, out):
    for c in range(0, out.shape[2], 128):
        part = slice(c, c + 128)
        keys = parts[0, :, part].astype(F32)
        for q in range(1, parts.shape[0]):
            keys += parts[q, :, part].astype(F32)
        error = (keys - targets[:, part].astype(F32)).astype(BF16)
        for q in range(out.shape[0]):
            out[q, :, part] = error


def term(blocks, errors, k, start, stop):
    ring, _, count, rows = blocks.shape
    return lax.dot_general(
        blocks[:, k].reshape(ring * count, rows),
        errors[:, :, start:stop].reshape(ring * count, stop - start),
        (((0,), (0,)), ((), ())),
        preferred_element_type=F32,
    )


def given_kernel(start, stop, blocks, errors, *rest):
    out = rest[-1]
    for i, k in enumerate((3, 1)):
        out[i] = term(blocks, errors, k, start, stop).astype(BF16)


def kept_kernel(start, stop, blocks, errors, _, across, own):
    across[...] = term(blocks, errors, 2, start, stop)
    own[...] = term(blocks, errors, 0, start, stop)


def across_kernel(kept, given, out):
    out[...] = (kept[...] + given[0].astype(F32)).astype(BF16)


def step_kernel(start, stop, kept, given, crossed, master, stepped, sent):
    grad = kept[...] + given[1].astype(F32) + crossed[...].astype(F32)
    new = master[:, start:stop] - (0.5 * SCALE) * grad
    stepped[...] = new
    sent[...] = new.astype(BF16)


def mean_kernel(start, stepped, other, *rest):
    out, held, sem = rest[-3:]
    held[...] = 0.5 * (stepped[...] + other[...].astype(F32))
    copy = pltpu.make_async_copy(held, out.at[:, pl.ds(start, held.shape[1])], sem)
    copy.start()
    copy.wait()


def from_behind(block, axis, distance):
    devices = range(lax.axis_size(axis))
    route = [((i - distance) % len(devices), i) for i in devices]
    return lax.ppermute(block, axis, route)


def body(master, features, targets):
    levels = lax.axis_size("rep").bit_length() - 1
    hop = 2 ** (STEP % levels)
    size = lax.axis_size("fsdp")
    ring = size // SIDE
    groups = [list(range(k, size, SIDE)) for k in range(SIDE)]

    def exchange(blocks):
        return lax.all_to_all(blocks, "fsdp", 0, 0, axis_index_groups=groups)

    def swap(block, k):
        return lax.ppermute(block, "fsdp", [(i, i ^ k) for i in range(size)])

    master, tokens, targets = master[0], features[0], targets[0]
    rows, width = master.shape
    count = tokens.shape[0]
    edges = [sum(PIECES[:h]) for h in range(len(PIECES) + 1)]
    chunks = list(zip(edges[:-1], edges[1:]))

    (working,) = call(round_kernel, "round", [((rows, width), BF16)], [VMEM])(master)
    beside = swap(working, 1)
    across = swap(working, 2)
    (working,) = call(stack_kernel, "stack", [((SIDE, rows, width), BF16)], [VMEM] * SIDE)(
        working, beside, across, swap(across, 1)
    )
    shape = (ring, SIDE, count, rows)
    blocks = pl.pallas_call(
        block_kernel,
        name="block",
        out_shape=jax.ShapeDtypeStruct(shape, BF16),
        in_specs=[pl.BlockSpec(memory_space=pl.ANY)],
        out_specs=pl.BlockSpec(memory_space=pl.ANY),
        scratch_shapes=[pltpu.VMEM((ring, count, SIDE * rows), BF16), pltpu.SemaphoreType.DMA((2, ring, SIDE))],
        compiler_params=pltpu.CompilerParams(vmem_limit_bytes=60 * 1024 * 1024),
    )(tokens)
    blocks = exchange(blocks)

    shape = (ring, count, width)
    (partial,) = call(keys_kernel, "keys", [(shape, BF16)], [VMEM] * 2)(blocks, working)
    (error,) = call(error_kernel, "error", [(shape, BF16)], [VMEM] * 2)(exchange(partial), targets)
    errors = exchange(error)

    results, after = [], []
    for h, (start, stop) in enumerate(chunks):
        half = (rows, stop - start)
        weight = max((len(chunks) - 1 - h) * FLOPS, 1_000_000)
        mean_weight = weight if len(chunks) == 2 else 1_000_000
        (given,) = call(
            functools.partial(given_kernel, start, stop),
            f"given_{h}",
            [((2, *half), BF16)],
            [VMEM] * 2 + [ANY] * len(after),
        )(blocks, errors, *after)
        across, kept = call(
            functools.partial(kept_kernel, start, stop),
            f"kept_{h}",
            [(half, F32)] * 2,
            [VMEM] * 2 + [ANY],
            KEPT[h],
        )(blocks, errors, given)
        given = swap(given, 1)
        (across,) = call(across_kernel, f"across_{h}", [(half, BF16)], [VMEM] * 2, weight)(
            across, given
        )
        after = [across]
        stepped, sent = call(
            functools.partial(step_kernel, start, stop),
            f"step_{h}",
            [(half, F32), (half, BF16)],
            [VMEM] * 4,
            weight,
        )(kept, given, swap(across, 2), master)
        results.append((start, half, mean_weight, stepped, from_behind(sent, "rep", hop)))
    updated = []
    for h, (start, half, weight, stepped, other) in enumerate(results):
        updated = pl.pallas_call(
            functools.partial(mean_kernel, start),
            name=f"mean_{h}",
            out_shape=[jax.ShapeDtypeStruct((rows, width), F32)],
            in_specs=[VMEM] * 2 + [ANY] * len(updated),
            out_specs=[ANY],
            scratch_shapes=[pltpu.VMEM(half, F32), pltpu.SemaphoreType.DMA],
            input_output_aliases={2: 0} if updated else {},
            compiler_params=pltpu.CompilerParams(vmem_limit_bytes=8 * 1024 * 1024),
            cost_estimate=pl.CostEstimate(flops=weight, bytes_accessed=1_000_000, transcendentals=0),
        )(stepped, other, *updated)
    (updated,) = updated
    return updated[None]


def solution(mesh):
    return jax.shard_map(
        body,
        mesh=mesh,
        in_specs=(P("rep", "fsdp", None), P("rep", "fsdp", None), P("rep", "fsdp", None)),
        out_specs=P("rep", "fsdp", None),
        check_vma=False,
    )
```
